512 devices in a mesh: redist: 64 (over z, y), contract: 8 (over x, core).
Axes of the slice: x: 4, y: 8, z: 8, core: 2. Of those that a mesh axis runs over, the one named last changes fastest.
Arguments:
- amplitudes: float32 [512, 8, 16384], P('redist', 'contract'), may hold values from -6 to 6
- integrals: float32 [8, 16384, 512], P('contract', 'redist'), may hold values from -0.0390625 to 0.0390625
- irrep_count: int32 [8], replicated, may hold values from 1 to 128, 900 in all
- pair_energy: float32 [512], P(('redist', 'contract')), may hold values from -2 to -0.5
- virt_energy: float32 [512], replicated, may hold values from 1 to 3
Outputs:
- delta: float32 [512, 512], P(('redist', 'contract'))
The draws below stay inside these ranges and needn't reach their ends.
Inputs may be any that keep to these rules, and one draw needn't show every extreme that they name: irrep_count[h] counts the virtual orbitals of irrep h; the counts sum to 900 and the largest is exactly 128.
All inputs are finite; a program needn't handle non-finite values.
Results may differ from the reference program's by a relative error of at most 0.0001.
Values sent between devices are 32-bit elements; how exact they have to be, the bound alone decides.
No kernel may reach another device: no remote copies, remote signals or barrier semaphores. Data moves between devices by JAX's collectives and lax.ppermute only.
A program may use at most 64 MiB of HBM per device.

```python
import math
import jax
import jax.numpy as jnp
import numpy as np
from jax import lax

NVIR = 900
NIRREP = 8
VMAX = 128
GAMMA = 3
AB = 512
PAIRS = 512


def steps_of(own_key, extent, split, smallest, high):
    def one(dim, parts):
        heights = jax.random.uniform(jax.random.fold_in(jax.random.fold_in(own_key, 6), dim), (parts,), jnp.float32, smallest / len(split), high / len(split))
        return jnp.repeat(jnp.exp(heights), extent[dim] // parts).reshape((-1,) + (1,) * (len(extent) - dim - 1))

    loudness = one(*split[0])
    for cut in split[1:]:
        loudness = loudness * one(*cut)
    return loudness


def profile(number_of, total, limit, skew):
    weights = [(1 << 20) // math.isqrt(grade ** skew) + 1 for grade in range(2, number_of + 1)]
    rest, given = total - limit - (number_of - 1), [1] * (number_of - 1)
    while rest > 0:
        candidates = [i for i in range(number_of - 1) if given[i] < limit]
        pool, remaining = sum([weights[i] for i in candidates]), rest
        for i in candidates:
            extra = min(limit - given[i], max(1, remaining * weights[i] // pool), rest)
            given[i] = given[i] + extra
            rest = rest - extra
    return np.array([limit] + given)


def ragged_sizes(key, amount, total, most, slope):
    if amount == 2:
        one = jax.random.randint(key, (), max(1, total - most), min(most, total - 1) + 1)
        return jnp.stack([one, total - one])
    sizes = jnp.asarray(profile(amount, total, most, slope), jnp.int32)
    couples = (amount - 1) // 2
    source_of, receiver = sizes[1:1 + 2 * couples:2], sizes[2:2 + 2 * couples:2]
    margin = jnp.minimum(source_of - 1, most - receiver)
    passed = jax.random.randint(jax.random.fold_in(key, 1), (couples,), 0, 1 << 20) % (margin + 1)
    sizes = sizes.at[1:1 + 2 * couples:2].set(source_of - passed).at[2:2 + 2 * couples:2].set(receiver + passed)
    return sizes[jax.random.permutation(jax.random.fold_in(key, 2), amount)]


def gaussian(rng, dims, spread, most, cuts=(), kind=jnp.bfloat16):
    result = jax.random.normal(rng, dims, jnp.float32) * spread
    if len(cuts) > 0:
        result = steps_of(rng, dims, cuts, -0.22, 0.18) * result
    return jnp.clip(result, min=-most, max=most).astype(kind)


def setup_inputs(seed: int = 0) -> dict:
    key_list = jax.random.split(jax.random.key(seed), 6)
    amplitudes = gaussian(key_list[0], (PAIRS, NIRREP, VMAX * VMAX), 1.0, 6.0, ((0, 64), (1, 8)), jnp.float32)
    integrals = gaussian(key_list[1], (NIRREP, VMAX * VMAX, AB), (NVIR * NVIR // 32) ** -0.5, 0.0390625, ((0, 8), (1, 64)), jnp.float32)
    irrep_count = ragged_sizes(key_list[2], NIRREP, NVIR, VMAX, 2).astype(jnp.int32)
    pair_energy = jnp.clip(-2.0 + 1.5 * jax.random.uniform(key_list[3], (PAIRS,), jnp.float32) ** steps_of(key_list[3], (PAIRS,), ((0, 512),), -0.2, 0.2), -2.0, -0.5)
    virt_energy = jnp.clip(jax.random.uniform(key_list[4], (AB,), jnp.float32, 1.0, 3.0), 1.0, 3.0)
    return dict(amplitudes=amplitudes, integrals=integrals, irrep_count=irrep_count, pair_energy=pair_energy, virt_energy=virt_energy)


def reference(amplitudes, integrals, irrep_count, pair_energy, virt_energy):
    irreps = jnp.arange(NIRREP, dtype=jnp.int32)
    partner = jnp.bitwise_xor(irreps, GAMMA)
    cell_index = jnp.arange(VMAX * VMAX, dtype=jnp.int32)
    row_index = cell_index // VMAX
    col_index = cell_index % VMAX
    live = ((row_index[None, :] < irrep_count[:, None]) & (col_index[None, :] < irrep_count[partner][:, None])).astype(jnp.float32)
    ladder = jnp.zeros((amplitudes.shape[0], integrals.shape[2]), jnp.float32)
    for irrep in range(NIRREP):
        masked = integrals[irrep] * (0.5 * live[irrep])[:, None]
        ladder = ladder + jnp.dot(amplitudes[:, irrep, :], masked, precision=lax.Precision.HIGHEST, preferred_element_type=jnp.float32)
    return ladder / (virt_energy[None, :] - pair_energy[:, None])
```

```python
import jax
import jax.numpy as jnp
from jax import lax
from jax.experimental import pallas as pl
from jax.experimental.pallas import tpu as pltpu
from jax.sharding import PartitionSpec as P

VMAX = 128
GAMMA = 3
VMEM_BYTES = 48 * 1024 * 1024


def regroup_kernel(cells_ref, out_ref):
    pairs, _, _ = cells_ref.shape
    slabs, lines, _ = out_ref.shape
    parts = lines // pairs
    for pair in range(pairs):
        for part in range(parts):
            out_ref[:, pair * parts + part, :] = cells_ref[pair, pl.ds(part, slabs, stride=parts), :]


def split_bf16(value):
    high = value.astype(jnp.bfloat16)
    return high, (value - high.astype(jnp.float32)).astype(jnp.bfloat16)


def ladder_kernel(count_ref, rows_ref, integrals_ref, out_ref):
    pairs, slabs, _ = out_ref.shape
    lines = rows_ref.shape[1]
    parts = lines // pairs
    irrep = lax.axis_index("contract")
    first_row = lax.axis_index("redist") * parts
    own_count = count_ref[irrep]
    partner_count = count_ref[jnp.bitwise_xor(irrep, GAMMA)]
    cells, _ = integrals_ref.shape
    cell = lax.broadcasted_iota(jnp.int32, integrals_ref.shape, 0)
    live = (first_row + cell // VMAX < own_count) & (cell % VMAX < partner_count)
    weights = jnp.where(live, 0.5 * integrals_ref[...], 0.0)
    rows = jnp.concatenate(
        [
            jnp.concatenate([rows_ref[:, pair * parts + part, :] for part in range(parts)], axis=1)
            for pair in range(pairs)
        ],
        axis=0,
    )
    total = jnp.dot(
        rows, weights, precision=lax.Precision.HIGHEST, preferred_element_type=jnp.float32
    )
    out_ref[...] = total.reshape(out_ref.shape)


def contract_sum_kernel(parts_ref, out_ref):
    total = jnp.sum(parts_ref[...], axis=0)
    slabs = total.shape[0]
    blocks = total.shape[1] // 128
    for block in range(blocks):
        out_ref[pl.ds(block, slabs, stride=blocks), :] = total[:, block * 128 : (block + 1) * 128]


def finish_kernel(pair_energy_ref, parts_ref, virt_energy_ref, out_ref):
    blocks = out_ref.shape[0]
    slabs = parts_ref.shape[0] // blocks
    total = jnp.concatenate(
        [
            jnp.sum(parts_ref[pl.ds(block, slabs, stride=blocks), :], axis=0, keepdims=True)
            for block in range(blocks)
        ],
        axis=0,
    )
    out_ref[...] = total / (virt_energy_ref[...] - pair_energy_ref[0])


def call(kernel, out_shape, in_memory):
    return pl.pallas_call(
        kernel,
        out_shape=jax.ShapeDtypeStruct(out_shape, jnp.float32),
        in_specs=[pl.BlockSpec(memory_space=space) for space in in_memory],
        out_specs=pl.BlockSpec(memory_space=pltpu.VMEM),
        compiler_params=pltpu.CompilerParams(vmem_limit_bytes=VMEM_BYTES),
    )


def body(amplitudes, integrals, irrep_count, pair_energy, virt_energy):
    slabs = lax.axis_size("redist")
    owners = lax.axis_size("contract")
    pairs, _, cells_all = amplitudes.shape
    _, cells, virt = integrals.shape
    parts = cells // VMAX
    vmem, smem = pltpu.VMEM, pltpu.SMEM

    grouped = call(regroup_kernel, (slabs, pairs * parts, VMAX), [vmem])(
        amplitudes.reshape(pairs, cells_all // VMAX, VMAX)
    )
    arrived = lax.all_to_all(grouped, "redist", split_axis=0, concat_axis=0, tiled=True)
    partial = call(ladder_kernel, (owners, slabs, virt), [smem, vmem, vmem])(
        irrep_count, arrived, integrals.reshape(cells, virt)
    )
    partial = lax.all_to_all(partial, "contract", split_axis=0, concat_axis=0, tiled=True)
    blocks = virt // 128
    summed = call(contract_sum_kernel, (slabs * blocks, 128), [vmem])(partial)
    summed = lax.all_to_all(
        summed.reshape(slabs, blocks, 128), "redist", split_axis=0, concat_axis=0, tiled=True
    )
    delta = call(finish_kernel, (blocks, 128), [smem, vmem, vmem])(
        pair_energy, summed.reshape(slabs * blocks, 128), virt_energy.reshape(blocks, 128)
    )
    return delta.reshape(1, virt)


def solution(mesh):
    in_specs = (
        P("redist", "contract", None),
        P("contract", "redist", None),
        P(),
        P(("redist", "contract")),
        P(),
    )
    out_specs = P(("redist", "contract"), None)
    return jax.shard_map(body, mesh=mesh, in_specs=in_specs, out_specs=out_specs, check_vma=False)
```

```python
import jax
import jax.numpy as jnp
from jax import lax
from jax.experimental import pallas as pl
from jax.experimental.pallas import tpu as pltpu
from jax.sharding import PartitionSpec as P

VMAX = 128
GAMMA = 3
CORES = 2
CHUNKS = 4
VMEM_BYTES = 48 * 1024 * 1024


def regroup_kernel(cells_ref, out_ref, held, ready, in_sems, out_sems):
    pairs, all_lines, _ = cells_ref.shape
    slabs, lines, _ = out_ref.shape
    parts = lines // pairs
    chunks = in_sems.shape[0]
    slabs_each, lines_each = slabs // chunks, all_lines // chunks
    arrivals = [
        pltpu.make_async_copy(
            cells_ref.at[:, pl.ds(chunk * lines_each, lines_each), :],
            held.at[chunk],
            in_sems.at[chunk],
        )
        for chunk in range(chunks)
    ]
    departures = [
        pltpu.make_async_copy(
            ready.at[chunk],
            out_ref.at[pl.ds(chunk * slabs_each, slabs_each)],
            out_sems.at[chunk],
        )
        for chunk in range(chunks)
    ]
    for arrival in arrivals:
        arrival.start()
    for chunk in range(chunks):
        arrivals[chunk].wait()
        for pair in range(pairs):
            line = (pair % CORES) * (lines // CORES) + (pair // CORES) * parts
            for part in range(parts):
                ready[chunk, :, line + part, :] = held[
                    chunk, pair, pl.ds(part, slabs_each, stride=parts), :
                ]
        departures[chunk].start()
    for departure in departures:
        departure.wait()


def split_bf16(value):
    high = value.astype(jnp.bfloat16)
    return high, (value - high.astype(jnp.float32)).astype(jnp.bfloat16)


def weights_kernel(
    count_ref, pair_energy_ref, own_ref, other_ref, virt_energy_ref, high_ref, low_ref, gap_ref
):
    cells, virt = own_ref.shape
    irrep = lax.axis_index("contract")
    core = irrep % CORES
    first_row = lax.axis_index("redist") * (cells // VMAX)
    cell = lax.broadcasted_iota(jnp.int32, (cells, virt), 0)
    row, col = first_row + cell // VMAX, cell % VMAX
    for source in range(CORES):
        owner = irrep - core + source
        live = (row < count_ref[owner]) & (col < count_ref[jnp.bitwise_xor(owner, GAMMA)])
        held = jnp.where(core == source, own_ref[...], other_ref[...])
        high, low = split_bf16(jnp.where(live, 0.5 * held, 0.0))
        high_ref[pl.ds(source * cells, cells), :] = high
        low_ref[pl.ds(source * cells, cells), :] = low
    gap_ref[...] = virt_energy_ref[...] - pair_energy_ref[0]


def ladder_kernel(rows_ref, high_ref, low_ref, out_ref):
    slabs, lines, _ = rows_ref.shape
    depth, virt = high_ref.shape
    blocks = virt // VMAX
    turns = out_ref.shape[1] // blocks
    pieces = depth // VMAX
    parts = pieces // CORES
    rows = jnp.concatenate(
        [
            jnp.concatenate(
                [
                    rows_ref[:, (source * turns + turn) * parts + part, :]
                    for source in range(CORES)
                    for part in range(parts)
                ],
                axis=1,
            )
            for turn in range(turns)
        ],
        axis=0,
    )
    rows_high, rows_low = split_bf16(rows)
    high, low = high_ref[...], low_ref[...]
    total = jnp.dot(rows_high, low, preferred_element_type=jnp.float32)
    total = total + jnp.dot(rows_low, high, preferred_element_type=jnp.float32)
    total = total + jnp.dot(rows_high, high, preferred_element_type=jnp.float32)
    for turn in range(turns):
        for block in range(blocks):
            out_ref[:, turn * blocks + block, :] = total[
                turn * slabs : (turn + 1) * slabs, block * VMAX : (block + 1) * VMAX
            ]


def finish_kernel(parts_ref, gap_ref, out_ref):
    blocks = out_ref.shape[0]
    total = jnp.sum(parts_ref[...].reshape(-1, 2 * blocks, VMAX), axis=0)
    out_ref[...] = (total[:blocks] + total[blocks:]) / gap_ref[...]


def call(kernel, outs, in_memory, cost=None, out_memory=pltpu.VMEM, scratch=()):
    single = not isinstance(outs, list)
    shapes = [jax.ShapeDtypeStruct(*out) for out in ([outs] if single else outs)]
    specs = [pl.BlockSpec(memory_space=out_memory) for _ in shapes]
    return pl.pallas_call(
        kernel,
        out_shape=shapes[0] if single else shapes,
        in_specs=[pl.BlockSpec(memory_space=space) for space in in_memory],
        out_specs=specs[0] if single else specs,
        scratch_shapes=scratch,
        cost_estimate=cost,
        compiler_params=pltpu.CompilerParams(vmem_limit_bytes=VMEM_BYTES),
    )


def body(amplitudes, integrals, irrep_count, pair_energy, virt_energy):
    slabs = lax.axis_size("redist")
    owners = lax.axis_size("contract")
    chips = owners // CORES
    pairs, _, cells_all = amplitudes.shape
    _, cells, virt = integrals.shape
    parts = cells // VMAX
    blocks = virt // VMAX
    vmem, smem, hbm = pltpu.VMEM, pltpu.SMEM, pltpu.HBM
    f32, bf16 = jnp.float32, jnp.bfloat16
    axes = ("redist", "contract")
    same_chips = [
        [slab * owners + chip * CORES + core for slab in range(slabs) for core in range(CORES)]
        for chip in range(chips)
    ]
    same_core = [
        [slab * owners + chip * CORES + core for slab in range(slabs) for chip in range(chips)]
        for core in range(CORES)
    ]

    lines = pairs * parts
    grouped = call(
        regroup_kernel,
        ((slabs, lines, VMAX), f32),
        [hbm],
        out_memory=hbm,
        scratch=[
            pltpu.VMEM((CHUNKS, pairs, parts * slabs // CHUNKS, VMAX), f32),
            pltpu.VMEM((CHUNKS, slabs // CHUNKS, lines, VMAX), f32),
            pltpu.SemaphoreType.DMA((CHUNKS,)),
            pltpu.SemaphoreType.DMA((CHUNKS,)),
        ],
    )(amplitudes.reshape(pairs, cells_all // VMAX, VMAX))
    arrived = lax.all_to_all(
        grouped.reshape(slabs * CORES, -1, VMAX),
        axes,
        split_axis=0,
        concat_axis=0,
        axis_index_groups=same_chips,
        tiled=True,
    ).reshape(slabs, lines, VMAX)

    own = integrals.reshape(cells, virt)
    other = lax.ppermute(own, "contract", [(owner, owner ^ 1) for owner in range(owners)])
    high, low, gap = call(
        weights_kernel,
        [((CORES * cells, virt), bf16), ((CORES * cells, virt), bf16), ((blocks, VMAX), f32)],
        [smem, smem, vmem, vmem, vmem],
        cost=pl.CostEstimate(flops=10 * CORES * cells * virt, bytes_accessed=8 * CORES * cells * virt, transcendentals=0),
    )(irrep_count, pair_energy, own, other, virt_energy.reshape(blocks, VMAX))

    partial = call(ladder_kernel, ((slabs, chips * blocks, VMAX), f32), [vmem] * 3)(
        arrived, high, low
    )
    partial = lax.all_to_all(
        partial.reshape(-1, blocks, VMAX),
        axes,
        split_axis=0,
        concat_axis=0,
        axis_index_groups=same_core,
        tiled=True,
    )
    delta = call(finish_kernel, ((blocks, VMAX), f32), [vmem] * 2)(
        partial.reshape(-1, VMAX), gap
    )
    return delta.reshape(1, virt)


def solution(mesh):
    in_specs = (
        P("redist", "contract", None),
        P("contract", "redist", None),
        P(),
        P(("redist", "contract")),
        P(),
    )
    out_specs = P(("redist", "contract"), None)
    return jax.shard_map(body, mesh=mesh, in_specs=in_specs, out_specs=out_specs, check_vma=False)
```

```python
import jax
import jax.numpy as jnp
from jax import lax
from jax.experimental import pallas as pl
from jax.experimental.pallas import tpu as pltpu
from jax.sharding import PartitionSpec as P

VMAX = 128
GAMMA = 3
CORES = 2
SLABS = 2
CHUNKS = 4
VMEM_BYTES = 48 * 1024 * 1024


def regroup_kernel(cells_ref, out_ref, ready, sems):
    pairs, all_lines, _ = cells_ref.shape
    places, lines, _ = out_ref.shape
    parts = lines // pairs
    chunks = sems.shape[0]
    places_each, lines_each = places // chunks, all_lines // chunks
    copies = []
    for chunk in range(chunks):
        for pair in range(pairs):
            line = (pair % CORES) * (lines // CORES) + (pair // CORES) * parts
            for part in range(parts):
                ready[chunk, :, line + part, :] = cells_ref[
                    pair, pl.ds(chunk * lines_each + part, places_each, stride=parts), :
                ]
        copies.append(
            pltpu.make_async_copy(
                ready.at[chunk],
                out_ref.at[pl.ds(chunk * places_each, places_each)],
                sems.at[chunk],
            )
        )
        copies[chunk].start()
    for copy in copies:
        copy.wait()


def split_bf16(value):
    high = value.astype(jnp.bfloat16)
    return high, (value - high.astype(jnp.float32)).astype(jnp.bfloat16)


def weights_kernel(count_ref, pair_energy_ref, virt_energy_ref, *refs):
    held_refs, (high_ref, low_ref, gap_ref) = refs[: CORES * SLABS], refs[CORES * SLABS :]
    cells, virt = held_refs[0].shape
    parts = cells // VMAX
    cell = lax.broadcasted_iota(jnp.int32, (cells, virt), 0)
    for turn, held_ref in enumerate(held_refs):
        irrep = jnp.bitwise_xor(lax.axis_index("contract"), turn // SLABS)
        slab = jnp.bitwise_xor(lax.axis_index("redist"), turn % SLABS)
        row, col = slab * parts + cell // VMAX, cell % VMAX
        live = (row < count_ref[irrep]) & (col < count_ref[jnp.bitwise_xor(irrep, GAMMA)])
        high, low = split_bf16(jnp.where(live, 0.5 * held_ref[...], 0.0))
        place = pl.multiple_of((irrep % CORES * SLABS + slab % SLABS) * cells, cells)
        high_ref[pl.ds(place, cells), :] = high
        low_ref[pl.ds(place, cells), :] = low
    gap_ref[...] = virt_energy_ref[...] - pair_energy_ref[0]


def ladder_kernel(rows_ref, high_ref, low_ref, out_ref):
    places, lines, _ = rows_ref.shape
    depth, virt = high_ref.shape
    blocks = virt // VMAX
    turns = out_ref.shape[1] // blocks
    parts = depth // VMAX // CORES
    rows = jnp.concatenate(
        [
            jnp.concatenate(
                [
                    rows_ref[:, (source * turns + turn) * parts + part, :]
                    for source in range(CORES)
                    for part in range(parts)
                ],
                axis=1,
            )
            for turn in range(turns)
        ],
        axis=0,
    )
    rows_high, rows_low = split_bf16(rows)
    high, low = high_ref[...], low_ref[...]
    total = jnp.dot(rows_high, low, preferred_element_type=jnp.float32)
    total = total + jnp.dot(rows_low, high, preferred_element_type=jnp.float32)
    total = total + jnp.dot(rows_high, high, preferred_element_type=jnp.float32)
    for turn in range(turns):
        for block in range(blocks):
            out_ref[:, turn * blocks + block, :] = total[
                turn * places : (turn + 1) * places, block * VMAX : (block + 1) * VMAX
            ]


def finish_kernel(parts_ref, gap_ref, out_ref):
    blocks = out_ref.shape[0]
    total = jnp.sum(parts_ref[...].reshape(-1, 2 * blocks, VMAX), axis=0)
    out_ref[...] = (total[:blocks] + total[blocks:]) / gap_ref[...]


def call(kernel, outs, in_memory, cost=None, out_memory=pltpu.VMEM, scratch=()):
    single = not isinstance(outs, list)
    shapes = [jax.ShapeDtypeStruct(*out) for out in ([outs] if single else outs)]
    specs = [pl.BlockSpec(memory_space=out_memory) for _ in shapes]
    return pl.pallas_call(
        kernel,
        out_shape=shapes[0] if single else shapes,
        in_specs=[pl.BlockSpec(memory_space=space) for space in in_memory],
        out_specs=specs[0] if single else specs,
        scratch_shapes=scratch,
        cost_estimate=cost,
        compiler_params=pltpu.CompilerParams(vmem_limit_bytes=VMEM_BYTES),
    )


def body(amplitudes, integrals, irrep_count, pair_energy, virt_energy):
    slabs = lax.axis_size("redist")
    owners = lax.axis_size("contract")
    pairs, _, cells_all = amplitudes.shape
    _, cells, virt = integrals.shape
    blocks = virt // VMAX
    places, chips = slabs // SLABS, owners // CORES
    vmem, smem = pltpu.VMEM, pltpu.SMEM
    f32, bf16 = jnp.float32, jnp.bfloat16

    def device(place, side, chip, core):
        slab = place * SLABS + (side ^ (place // 2 % 2))
        return slab * owners + chip * CORES + core

    same_chip = [
        [device(place, side, chip, core) for place in range(places) for core in range(CORES)]
        for side in range(SLABS)
        for chip in range(chips)
    ]
    same_core = [
        [device(place, side, chip, core) for place in range(places) for chip in range(chips)]
        for side in range(SLABS)
        for core in range(CORES)
    ]

    def exchange(blocks_out, groups):
        return lax.all_to_all(
            blocks_out,
            ("redist", "contract"),
            split_axis=0,
            concat_axis=0,
            axis_index_groups=groups,
            tiled=True,
        )

    def swap(block, axis):
        count = lax.axis_size(axis)
        return lax.ppermute(block, axis, [(index, index ^ 1) for index in range(count)])

    own = integrals.reshape(cells, virt)
    held = [own, swap(own, "redist")]
    held = held + [swap(block, "contract") for block in held]

    all_lines = cells_all // VMAX
    lines = pairs * all_lines // places
    grouped = call(
        regroup_kernel,
        ((places, lines, VMAX), f32),
        [vmem],
        out_memory=pltpu.HBM,
        scratch=[
            pltpu.VMEM((CHUNKS, places // CHUNKS, lines, VMAX), f32),
            pltpu.SemaphoreType.DMA((CHUNKS,)),
        ],
    )(amplitudes.reshape(pairs, all_lines, VMAX))
    arrived = exchange(grouped.reshape(places * CORES, lines // CORES, VMAX), same_chip)

    depth = CORES * SLABS * cells
    high, low, gap = call(
        weights_kernel,
        [((depth, virt), bf16), ((depth, virt), bf16), ((blocks, VMAX), f32)],
        [smem, smem, vmem] + [vmem] * len(held),
        cost=pl.CostEstimate(
            flops=10 * depth * virt, bytes_accessed=8 * depth * virt, transcendentals=0
        ),
    )(irrep_count, pair_energy, virt_energy.reshape(blocks, VMAX), *held)

    partial = call(ladder_kernel, ((places, chips * blocks, VMAX), f32), [vmem] * 3)(
        arrived.reshape(places, lines, VMAX), high, low
    )
    partial = exchange(partial.reshape(places * chips, blocks, VMAX), same_core)
    delta = call(finish_kernel, ((blocks, VMAX), f32), [vmem] * 2)(
        partial.reshape(-1, VMAX), gap
    )
    return delta.reshape(1, virt)


def solution(mesh):
    in_specs = (
        P("redist", "contract", None),
        P("contract", "redist", None),
        P(),
        P(("redist", "contract")),
        P(),
    )
    out_specs = P(("redist", "contract"), None)
    return jax.shard_map(body, mesh=mesh, in_specs=in_specs, out_specs=out_specs, check_vma=False)
```

```python
import functools

import jax
import jax.numpy as jnp
from jax import lax
from jax.experimental import pallas as pl
from jax.experimental.pallas import tpu as pltpu
from jax.sharding import PartitionSpec as P

VMAX = 128
GAMMA = 3
CORES = 2
SLABS = 2
CHUNKS = 4
RING = 8
VMEM_BYTES = 48 * 1024 * 1024


def first_swapped(count, first):
    order = list(range(count))
    order[0], order[first] = first, 0
    return order


def regroup_kernel(place_order, cells_ref, out_ref, ready, sems):
    pairs, all_lines, _ = cells_ref.shape
    places, lines, _ = out_ref.shape
    parts = lines // pairs
    chunks = sems.shape[0]
    places_each, lines_each = places // chunks, all_lines // chunks
    copies = []
    for chunk in range(chunks):
        for pair in range(pairs):
            line = (pair % CORES) * (lines // CORES) + (pair // CORES) * parts
            for part in range(parts):
                ready[chunk, :, line + part, :] = cells_ref[
                    pair, pl.ds(chunk * lines_each + part, places_each, stride=parts), :
                ]
            for index in range(places_each):
                place = place_order[chunk * places_each + index]
                if place != chunk * places_each + index:
                    ready[chunk, index, line : line + parts, :] = cells_ref[
                        pair, place * parts : (place + 1) * parts, :
                    ]
        copies.append(
            pltpu.make_async_copy(
                ready.at[chunk],
                out_ref.at[pl.ds(chunk * places_each, places_each)],
                sems.at[chunk],
            )
        )
        copies[chunk].start()
    for copy in copies:
        copy.wait()


def split_bf16(value):
    high = value.astype(jnp.bfloat16)
    return high, (value - high.astype(jnp.float32)).astype(jnp.bfloat16)


def weights_kernel(count_ref, pair_energy_ref, virt_energy_ref, *refs):
    held_refs, (high_ref, low_ref, gap_ref) = refs[: CORES * SLABS], refs[CORES * SLABS :]
    cells, virt = held_refs[0].shape
    parts = cells // VMAX
    cell = lax.broadcasted_iota(jnp.int32, (cells, virt), 0)
    for turn, held_ref in enumerate(held_refs):
        irrep = jnp.bitwise_xor(lax.axis_index("contract"), turn // SLABS)
        slab = jnp.bitwise_xor(lax.axis_index("redist"), turn % SLABS)
        row, col = slab * parts + cell // VMAX, cell % VMAX
        live = (row < count_ref[irrep]) & (col < count_ref[jnp.bitwise_xor(irrep, GAMMA)])
        high, low = split_bf16(jnp.where(live, 0.5 * held_ref[...], 0.0))
        place = pl.multiple_of((irrep % CORES * SLABS + slab % SLABS) * cells, cells)
        high_ref[pl.ds(place, cells), :] = high
        low_ref[pl.ds(place, cells), :] = low
    gap_ref[...] = virt_energy_ref[...] - pair_energy_ref[0]


def ladder_kernel(chip_order, rows_ref, high_ref, low_ref, out_ref):
    places, lines, _ = rows_ref.shape
    depth, virt = high_ref.shape
    blocks = virt // VMAX
    turns = out_ref.shape[1] // blocks
    parts = depth // VMAX // CORES
    rows = jnp.concatenate(
        [
            jnp.concatenate(
                [
                    rows_ref[:, (source * turns + turn) * parts + part, :]
                    for source in range(CORES)
                    for part in range(parts)
                ],
                axis=1,
            )
            for turn in range(turns)
        ],
        axis=0,
    )
    rows_high, rows_low = split_bf16(rows)
    high, low = high_ref[...], low_ref[...]
    total = jnp.dot(rows_high, low, preferred_element_type=jnp.float32)
    total = total + jnp.dot(rows_low, high, preferred_element_type=jnp.float32)
    total = total + jnp.dot(rows_high, high, preferred_element_type=jnp.float32)
    for index, turn in enumerate(chip_order):
        for block in range(blocks):
            out_ref[:, index * blocks + block, :] = total[
                turn * places : (turn + 1) * places, block * VMAX : (block + 1) * VMAX
            ]


def finish_kernel(parts_ref, gap_ref, out_ref):
    blocks = out_ref.shape[0]
    total = jnp.sum(parts_ref[...].reshape(-1, 2 * blocks, VMAX), axis=0)
    out_ref[...] = (total[:blocks] + total[blocks:]) / gap_ref[...]


def call(kernel, outs, in_memory, cost=None, out_memory=pltpu.VMEM, scratch=()):
    single = not isinstance(outs, list)
    shapes = [jax.ShapeDtypeStruct(*out) for out in ([outs] if single else outs)]
    specs = [pl.BlockSpec(memory_space=out_memory) for _ in shapes]
    return pl.pallas_call(
        kernel,
        out_shape=shapes[0] if single else shapes,
        in_specs=[pl.BlockSpec(memory_space=space) for space in in_memory],
        out_specs=specs[0] if single else specs,
        scratch_shapes=scratch,
        cost_estimate=cost,
        compiler_params=pltpu.CompilerParams(vmem_limit_bytes=VMEM_BYTES),
    )


def body(amplitudes, integrals, irrep_count, pair_energy, virt_energy):
    slabs = lax.axis_size("redist")
    owners = lax.axis_size("contract")
    pairs, _, cells_all = amplitudes.shape
    _, cells, virt = integrals.shape
    blocks = virt // VMAX
    places, chips = slabs // SLABS, owners // CORES
    vmem, smem = pltpu.VMEM, pltpu.SMEM
    f32, bf16 = jnp.float32, jnp.bfloat16

    def device(place, side, chip, core):
        slab = place * SLABS + (side ^ (place // 2 % 2))
        return slab * owners + chip * CORES + core

    columns = RING // SLABS
    place_order = first_swapped(places, places // 2 + columns // 2)
    chip_order = first_swapped(chips, chips // 2)
    same_chip = [
        [device(place, side, chip, core) for place in place_order for core in range(CORES)]
        for side in range(SLABS)
        for chip in range(chips)
    ]
    same_core = [
        [device(place, side, chip, core) for place in place_order for chip in chip_order]
        for side in range(SLABS)
        for core in range(CORES)
    ]

    def exchange(blocks_out, groups):
        return lax.all_to_all(
            blocks_out,
            ("redist", "contract"),
            split_axis=0,
            concat_axis=0,
            axis_index_groups=groups,
            tiled=True,
        )

    def swap(block, axis):
        count = lax.axis_size(axis)
        return lax.ppermute(block, axis, [(index, index ^ 1) for index in range(count)])

    own = integrals.reshape(cells, virt)
    held = [own, swap(own, "redist")]
    held = held + [swap(block, "contract") for block in held]

    all_lines = cells_all // VMAX
    lines = pairs * all_lines // places
    grouped = call(
        functools.partial(regroup_kernel, place_order),
        ((places, lines, VMAX), f32),
        [vmem],
        out_memory=pltpu.HBM,
        scratch=[
            pltpu.VMEM((CHUNKS, places // CHUNKS, lines, VMAX), f32),
            pltpu.SemaphoreType.DMA((CHUNKS,)),
        ],
    )(amplitudes.reshape(pairs, all_lines, VMAX))
    arrived = exchange(grouped.reshape(places * CORES, lines // CORES, VMAX), same_chip)

    depth = CORES * SLABS * cells
    high, low, gap = call(
        weights_kernel,
        [((depth, virt), bf16), ((depth, virt), bf16), ((blocks, VMAX), f32)],
        [smem, smem, vmem] + [vmem] * len(held),
        cost=pl.CostEstimate(
            flops=10 * depth * virt, bytes_accessed=8 * depth * virt, transcendentals=0
        ),
    )(irrep_count, pair_energy, virt_energy.reshape(blocks, VMAX), *held)

    partial = call(
        functools.partial(ladder_kernel, chip_order),
        ((places, chips * blocks, VMAX), f32),
        [vmem] * 3,
    )(arrived.reshape(places, lines, VMAX), high, low)
    partial = exchange(partial.reshape(places * chips, blocks, VMAX), same_core)
    delta = call(finish_kernel, ((blocks, VMAX), f32), [vmem] * 2)(
        partial.reshape(-1, VMAX), gap
    )
    return delta.reshape(1, virt)


def solution(mesh):
    in_specs = (
        P("redist", "contract", None),
        P("contract", "redist", None),
        P(),
        P(("redist", "contract")),
        P(),
    )
    out_specs = P(("redist", "contract"), None)
    return jax.shard_map(body, mesh=mesh, in_specs=in_specs, out_specs=out_specs, check_vma=False)
```

```python
import functools

import jax
import jax.numpy as jnp
from jax import lax
from jax.experimental import pallas as pl
from jax.experimental.pallas import tpu as pltpu
from jax.sharding import PartitionSpec as P

VMAX = 128
GAMMA = 3
CORES = 2
SLABS = 2
RING = 8
VMEM_BYTES = 48 * 1024 * 1024


def first_swapped(count, first):
    order = list(range(count))
    order[0], order[first] = first, 0
    return order


def regroup_kernel(place_order, cells_ref, out_ref, ready, sems):
    pairs = cells_ref.shape[0]
    rows, columns, lines, _ = ready.shape
    parts = lines // pairs // SLABS
    copies = []
    for row in range(rows):
        for pair in range(pairs):
            for side in range(SLABS):
                line = ((pair % CORES * pairs + pair // CORES * CORES) // CORES * SLABS + side) * parts
                first = (row * SLABS + side) * columns * parts
                for part in range(parts):
                    ready[row, :, line + part, :] = cells_ref[
                        pair, pl.ds(first + part, columns, stride=parts), :
                    ]
                for index in range(columns):
                    place = place_order[row * columns + index]
                    if place != row * columns + index:
                        slab = (place // columns * SLABS + side) * columns + place % columns
                        ready[row, index, line : line + parts, :] = cells_ref[
                            pair, slab * parts : (slab + 1) * parts, :
                        ]
        copies.append(
            pltpu.make_async_copy(
                ready.at[row], out_ref.at[pl.ds(row * columns, columns)], sems.at[row]
            )
        )
        copies[row].start()
    for copy in copies:
        copy.wait()


def split_bf16(value):
    high = value.astype(jnp.bfloat16)
    return high, (value - high.astype(jnp.float32)).astype(jnp.bfloat16)


def put_weights(moves, count_ref, held_refs, high_ref, low_ref):
    for (core_move, slab_move), held_ref in zip(moves, held_refs):
        cells, virt = held_ref.shape
        irrep = jnp.bitwise_xor(lax.axis_index("contract"), core_move)
        slab = jnp.bitwise_xor(lax.axis_index("redist"), slab_move)
        cell = lax.broadcasted_iota(jnp.int32, (cells, virt), 0)
        row, col = slab * (cells // VMAX) + cell // VMAX, cell % VMAX
        live = (row < count_ref[irrep]) & (col < count_ref[jnp.bitwise_xor(irrep, GAMMA)])
        high, low = split_bf16(jnp.where(live, 0.5 * held_ref[...], 0.0))
        block = irrep % CORES * SLABS + slab // RING % SLABS
        place = pl.multiple_of(block * cells, cells)
        high_ref[pl.ds(place, cells), :] = high
        low_ref[pl.ds(place, cells), :] = low


def weights_kernel(moves, count_ref, pair_energy_ref, virt_energy_ref, *refs):
    held_refs, (high_ref, low_ref, gap_ref) = refs[: len(moves)], refs[len(moves) :]
    put_weights(moves, count_ref, held_refs, high_ref, low_ref)
    gap_ref[...] = virt_energy_ref[...] - pair_energy_ref[0]


def last_weights_kernel(move, count_ref, held_ref, _, __, high_ref, low_ref):
    put_weights([move], count_ref, [held_ref], high_ref, low_ref)


def ladder_kernel(chip_order, rows_ref, high_ref, low_ref, out_ref):
    places, lines, _ = rows_ref.shape
    depth, virt = high_ref.shape
    blocks = virt // VMAX
    turns = out_ref.shape[1] // blocks
    parts = depth // VMAX // CORES
    rows = jnp.concatenate(
        [
            jnp.concatenate(
                [
                    rows_ref[:, (source * turns + turn) * parts + part, :]
                    for source in range(CORES)
                    for part in range(parts)
                ],
                axis=1,
            )
            for turn in range(turns)
        ],
        axis=0,
    )
    rows_high, rows_low = split_bf16(rows)
    high, low = high_ref[...], low_ref[...]
    total = jnp.dot(rows_high, low, preferred_element_type=jnp.float32)
    total = total + jnp.dot(rows_low, high, preferred_element_type=jnp.float32)
    total = total + jnp.dot(rows_high, high, preferred_element_type=jnp.float32)
    for index, turn in enumerate(chip_order):
        for block in range(blocks):
            out_ref[:, index * blocks + block, :] = total[
                turn * places : (turn + 1) * places, block * VMAX : (block + 1) * VMAX
            ]


def finish_kernel(parts_ref, gap_ref, out_ref):
    blocks = out_ref.shape[0]
    total = jnp.sum(parts_ref[...].reshape(-1, 2 * blocks, VMAX), axis=0)
    out_ref[...] = (total[:blocks] + total[blocks:]) / gap_ref[...]


def call(kernel, outs, in_memory, cost=None, out_memory=pltpu.VMEM, scratch=(), aliases={}):
    single = not isinstance(outs, list)
    shapes = [jax.ShapeDtypeStruct(*out) for out in ([outs] if single else outs)]
    specs = [pl.BlockSpec(memory_space=out_memory) for _ in shapes]
    return pl.pallas_call(
        kernel,
        out_shape=shapes[0] if single else shapes,
        in_specs=[pl.BlockSpec(memory_space=space) for space in in_memory],
        out_specs=specs[0] if single else specs,
        scratch_shapes=scratch,
        cost_estimate=cost,
        input_output_aliases=aliases,
        compiler_params=pltpu.CompilerParams(vmem_limit_bytes=VMEM_BYTES),
    )


def body(amplitudes, integrals, irrep_count, pair_energy, virt_energy):
    slabs = lax.axis_size("redist")
    owners = lax.axis_size("contract")
    pairs, _, cells_all = amplitudes.shape
    _, cells, virt = integrals.shape
    blocks = virt // VMAX
    places, chips = slabs // SLABS, owners // CORES
    vmem, smem = pltpu.VMEM, pltpu.SMEM
    f32, bf16 = jnp.float32, jnp.bfloat16

    def device(place, side, chip, core):
        row, column = divmod(place, RING)
        slab = (row * SLABS + (side ^ ((row + 1) // 2 % 2))) * RING + column
        return slab * owners + chip * CORES + core

    rows = places // RING
    place_order = first_swapped(places, rows // 2 * RING + RING // 2)
    chip_order = first_swapped(chips, chips // 2)
    same_chip = [
        [device(place, side, chip, core) for place in place_order for core in range(CORES)]
        for side in range(SLABS)
        for chip in range(chips)
    ]
    same_core = [
        [device(place, side, chip, core) for place in place_order for chip in chip_order]
        for side in range(SLABS)
        for core in range(CORES)
    ]

    def exchange(blocks_out, groups):
        return lax.all_to_all(
            blocks_out,
            ("redist", "contract"),
            split_axis=0,
            concat_axis=0,
            axis_index_groups=groups,
            tiled=True,
        )

    def swap(block, axis, move):
        count = lax.axis_size(axis)
        return lax.ppermute(block, axis, [(index, index ^ move) for index in range(count)])

    own = integrals.reshape(cells, virt)
    held = {(0, 0): own, (0, RING): swap(own, "redist", RING)}
    held |= {(1, move): swap(block, "contract", 1) for (_, move), block in held.items()}
    last_move, last_block = held.popitem()

    all_lines = cells_all // VMAX
    lines = pairs * all_lines // places
    grouped = call(
        functools.partial(regroup_kernel, place_order),
        ((places, lines, VMAX), f32),
        [vmem],
        out_memory=pltpu.HBM,
        scratch=[
            pltpu.VMEM((rows, RING, lines, VMAX), f32),
            pltpu.SemaphoreType.DMA((rows,)),
        ],
    )(amplitudes.reshape(pairs, all_lines, VMAX))
    arrived = exchange(grouped.reshape(places * CORES, lines // CORES, VMAX), same_chip)

    depth = CORES * SLABS * cells
    weights = ((depth, virt), bf16)

    def cost(blocks_made):
        amount = blocks_made * cells * virt
        return pl.CostEstimate(flops=10 * amount, bytes_accessed=8 * amount, transcendentals=0)

    high, low, gap = call(
        functools.partial(weights_kernel, list(held)),
        [weights, weights, ((blocks, VMAX), f32)],
        [smem, smem, vmem] + [vmem] * len(held),
        cost=cost(len(held)),
    )(irrep_count, pair_energy, virt_energy.reshape(blocks, VMAX), *held.values())
    high, low = call(
        functools.partial(last_weights_kernel, last_move),
        [weights, weights],
        [smem, vmem, vmem, vmem],
        cost=cost(1),
        aliases={2: 0, 3: 1},
    )(irrep_count, last_block, high, low)

    partial = call(
        functools.partial(ladder_kernel, chip_order),
        ((places, chips * blocks, VMAX), f32),
        [vmem] * 3,
    )(arrived.reshape(places, lines, VMAX), high, low)
    partial = exchange(partial.reshape(places * chips, blocks, VMAX), same_core)
    delta = call(finish_kernel, ((blocks, VMAX), f32), [vmem] * 2)(
        partial.reshape(-1, VMAX), gap
    )
    return delta.reshape(1, virt)


def solution(mesh):
    in_specs = (
        P("redist", "contract", None),
        P("contract", "redist", None),
        P(),
        P(("redist", "contract")),
        P(),
    )
    out_specs = P(("redist", "contract"), None)
    return jax.shard_map(body, mesh=mesh, in_specs=in_specs, out_specs=out_specs, check_vma=False)
```

```python
import functools

import jax
import jax.numpy as jnp
from jax import lax
from jax.experimental import pallas as pl
from jax.experimental.pallas import tpu as pltpu
from jax.sharding import PartitionSpec as P

VMAX = 128
GAMMA = 3
CORES = 2
SLABS = 2
RING = 8
VMEM_BYTES = 48 * 1024 * 1024


def first_swapped(count, first):
    order = list(range(count))
    order[0], order[first] = first, 0
    return order


def regroup_kernel(place_order, cells_ref, out_ref, ready, sems):
    pairs = cells_ref.shape[0]
    rows, columns, lines, _ = ready.shape
    parts = lines // pairs // SLABS
    copies = []
    for row in range(rows):
        for pair in range(pairs):
            for side in range(SLABS):
                line = ((pair % CORES * pairs + pair // CORES * CORES) // CORES * SLABS + side) * parts
                first = (row * SLABS + side) * columns * parts
                for part in range(parts):
                    ready[row, :, line + part, :] = cells_ref[
                        pair, pl.ds(first + part, columns, stride=parts), :
                    ]
                for index in range(columns):
                    place = place_order[row * columns + index]
                    if place != row * columns + index:
                        slab = (place // columns * SLABS + side) * columns + place % columns
                        ready[row, index, line : line + parts, :] = cells_ref[
                            pair, slab * parts : (slab + 1) * parts, :
                        ]
        copies.append(
            pltpu.make_async_copy(
                ready.at[row], out_ref.at[pl.ds(row * columns, columns)], sems.at[row]
            )
        )
        copies[row].start()
    for copy in copies:
        copy.wait()


def split_bf16(value):
    high = value.astype(jnp.bfloat16)
    return high, (value - high.astype(jnp.float32)).astype(jnp.bfloat16)


def put_weights(moves, count_ref, held_refs, high_ref, low_ref):
    for index, ((core_move, slab_move), held_ref) in enumerate(zip(moves, held_refs)):
        cells, virt = held_ref.shape
        irrep = jnp.bitwise_xor(lax.axis_index("contract"), core_move)
        slab = jnp.bitwise_xor(lax.axis_index("redist"), slab_move)
        cell = lax.broadcasted_iota(jnp.int32, (cells, virt), 0)
        row, col = slab * (cells // VMAX) + cell // VMAX, cell % VMAX
        live = (row < count_ref[irrep]) & (col < count_ref[jnp.bitwise_xor(irrep, GAMMA)])
        high, low = split_bf16(jnp.where(live, 0.5 * held_ref[...], 0.0))
        high_ref[index * cells : (index + 1) * cells, :] = high
        low_ref[index * cells : (index + 1) * cells, :] = low


def weights_kernel(moves, count_ref, pair_energy_ref, virt_energy_ref, *refs):
    held_refs, (high_ref, low_ref, gap_ref) = refs[: len(moves)], refs[len(moves) :]
    put_weights(moves, count_ref, held_refs, high_ref, low_ref)
    gap_ref[...] = virt_energy_ref[...] - pair_energy_ref[0]


def last_weights_kernel(move, count_ref, held_ref, high_ref, low_ref):
    put_weights([move], count_ref, [held_ref], high_ref, low_ref)


def ladder_kernel(chip_order, moves, rows_ref, high_ref, low_ref, last_high_ref, last_low_ref, out_ref):
    places, lines, _ = rows_ref.shape
    virt = high_ref.shape[1]
    blocks = virt // VMAX
    turns = out_ref.shape[1] // blocks
    parts = last_high_ref.shape[0] // VMAX
    core = lax.axis_index("contract") % CORES
    side = lax.axis_index("redist") // RING % SLABS

    def arrived(source, slab_side):
        return jnp.concatenate(
            [
                jnp.concatenate(
                    [
                        rows_ref[:, ((source * turns + turn) * SLABS + slab_side) * parts + part, :]
                        for part in range(parts)
                    ],
                    axis=1,
                )
                for turn in range(turns)
            ],
            axis=0,
        )

    by_source = [[arrived(source, slab_side) for slab_side in range(SLABS)] for source in range(CORES)]
    by_core = [
        [jnp.where(core == 0, by_source[turn][place], by_source[1 - turn][place]) for place in range(SLABS)]
        for turn in range(CORES)
    ]
    by_move = {
        (turn, place * RING): jnp.where(side == 0, by_core[turn][place], by_core[turn][1 - place])
        for turn in range(CORES)
        for place in range(SLABS)
    }
    pieces = [by_move[move] for move in moves]
    total = jnp.zeros((turns * places, virt), jnp.float32)
    for rows, high, low in (
        (pieces[-1], last_high_ref[...], last_low_ref[...]),
        (jnp.concatenate(pieces[:-1], axis=1), high_ref[...], low_ref[...]),
    ):
        rows_high, rows_low = split_bf16(rows)
        total = total + jnp.dot(rows_high, low, preferred_element_type=jnp.float32)
        total = total + jnp.dot(rows_low, high, preferred_element_type=jnp.float32)
        total = total + jnp.dot(rows_high, high, preferred_element_type=jnp.float32)
    for index, turn in enumerate(chip_order):
        for block in range(blocks):
            out_ref[:, index * blocks + block, :] = total[
                turn * places : (turn + 1) * places, block * VMAX : (block + 1) * VMAX
            ]


def finish_kernel(parts_ref, gap_ref, out_ref):
    blocks = out_ref.shape[0]
    total = jnp.sum(parts_ref[...].reshape(-1, 2 * blocks, VMAX), axis=0)
    out_ref[...] = (total[:blocks] + total[blocks:]) / gap_ref[...]


def call(kernel, outs, in_memory, cost=None, out_memory=pltpu.VMEM, scratch=()):
    single = not isinstance(outs, list)
    shapes = [jax.ShapeDtypeStruct(*out) for out in ([outs] if single else outs)]
    specs = [pl.BlockSpec(memory_space=out_memory) for _ in shapes]
    return pl.pallas_call(
        kernel,
        out_shape=shapes[0] if single else shapes,
        in_specs=[pl.BlockSpec(memory_space=space) for space in in_memory],
        out_specs=specs[0] if single else specs,
        scratch_shapes=scratch,
        cost_estimate=cost,
        compiler_params=pltpu.CompilerParams(vmem_limit_bytes=VMEM_BYTES),
    )


def body(amplitudes, integrals, irrep_count, pair_energy, virt_energy):
    slabs = lax.axis_size("redist")
    owners = lax.axis_size("contract")
    pairs, _, cells_all = amplitudes.shape
    _, cells, virt = integrals.shape
    blocks = virt // VMAX
    places, chips = slabs // SLABS, owners // CORES
    vmem, smem = pltpu.VMEM, pltpu.SMEM
    f32, bf16 = jnp.float32, jnp.bfloat16

    def device(place, side, chip, core):
        row, column = divmod(place, RING)
        slab = (row * SLABS + (side ^ ((row + 1) // 2 % 2))) * RING + column
        return slab * owners + chip * CORES + core

    rows = places // RING
    place_order = first_swapped(places, rows // 2 * RING + RING // 2)
    chip_order = first_swapped(chips, chips // 2)
    same_chip = [
        [device(place, side, chip, core) for place in place_order for core in range(CORES)]
        for side in range(SLABS)
        for chip in range(chips)
    ]
    same_core = [
        [device(place, side, chip, core) for place in place_order for chip in chip_order]
        for side in range(SLABS)
        for core in range(CORES)
    ]

    def exchange(blocks_out, groups):
        return lax.all_to_all(
            blocks_out,
            ("redist", "contract"),
            split_axis=0,
            concat_axis=0,
            axis_index_groups=groups,
            tiled=True,
        )

    def swap(block, axis, move):
        count = lax.axis_size(axis)
        return lax.ppermute(block, axis, [(index, index ^ move) for index in range(count)])

    own = integrals.reshape(cells, virt)
    held = {(0, 0): own, (0, RING): swap(own, "redist", RING)}
    held |= {(1, move): swap(block, "contract", 1) for (_, move), block in held.items()}
    last_move, last_block = held.popitem()

    all_lines = cells_all // VMAX
    lines = pairs * all_lines // places
    grouped = call(
        functools.partial(regroup_kernel, place_order),
        ((places, lines, VMAX), f32),
        [vmem],
        out_memory=pltpu.HBM,
        scratch=[
            pltpu.VMEM((rows, RING, lines, VMAX), f32),
            pltpu.SemaphoreType.DMA((rows,)),
        ],
    )(amplitudes.reshape(pairs, all_lines, VMAX))
    arrived = exchange(grouped.reshape(places * CORES, lines // CORES, VMAX), same_chip)

    def weights(blocks_made):
        amount = blocks_made * cells * virt
        return (
            [((blocks_made * cells, virt), bf16)] * 2,
            pl.CostEstimate(flops=10 * amount, bytes_accessed=8 * amount, transcendentals=0),
        )

    outs, cost = weights(len(held))
    high, low, gap = call(
        functools.partial(weights_kernel, list(held)),
        [*outs, ((blocks, VMAX), f32)],
        [smem, smem, vmem] + [vmem] * len(held),
        cost=cost,
    )(irrep_count, pair_energy, virt_energy.reshape(blocks, VMAX), *held.values())
    outs, cost = weights(1)
    last_high, last_low = call(
        functools.partial(last_weights_kernel, last_move), outs, [smem, vmem], cost=cost
    )(irrep_count, last_block)

    partial = call(
        functools.partial(ladder_kernel, chip_order, [*held, last_move]),
        ((places, chips * blocks, VMAX), f32),
        [vmem] * 5,
    )(arrived.reshape(places, lines, VMAX), high, low, last_high, last_low)
    partial = exchange(partial.reshape(places * chips, blocks, VMAX), same_core)
    delta = call(finish_kernel, ((blocks, VMAX), f32), [vmem] * 2)(
        partial.reshape(-1, VMAX), gap
    )
    return delta.reshape(1, virt)


def solution(mesh):
    in_specs = (
        P("redist", "contract", None),
        P("contract", "redist", None),
        P(),
        P(("redist", "contract")),
        P(),
    )
    out_specs = P(("redist", "contract"), None)
    return jax.shard_map(body, mesh=mesh, in_specs=in_specs, out_specs=out_specs, check_vma=False)
```

```python
import functools

import jax
import jax.numpy as jnp
from jax import lax
from jax.experimental import pallas as pl
from jax.experimental.pallas import tpu as pltpu
from jax.sharding import PartitionSpec as P

VMAX = 128
GAMMA = 3
CORES = 2
SLABS = 2
RING = 8
VMEM_BYTES = 48 * 1024 * 1024
ALL_VMEM_BYTES = 63000000


def first_swapped(count, first):
    order = list(range(count))
    order[0], order[first] = first, 0
    return order


def regroup_kernel(place_order, cells_ref, out_ref, held, ready, in_sems, out_sems):
    pairs = cells_ref.shape[0]
    rows, columns, lines, _ = ready.shape
    parts = lines // pairs // SLABS
    row_lines = SLABS * columns * parts
    arrivals = [
        pltpu.make_async_copy(
            cells_ref.at[:, pl.ds(row * row_lines, row_lines), :], held.at[row], in_sems.at[row]
        )
        for row in range(rows)
    ]
    swapped = [row for row in range(rows) if place_order[row * columns] != row * columns]
    swapped += [place_order[row * columns] // columns for row in swapped]
    turns = sorted(range(rows), key=lambda row: row in swapped)
    for row in turns:
        arrivals[row].start()
    copies, waited = [], set()
    for row in turns:
        for needed in swapped if row in swapped else [row]:
            if needed not in waited:
                arrivals[needed].wait()
                waited.add(needed)
        for pair in range(pairs):
            for side in range(SLABS):
                line = ((pair % CORES * pairs + pair // CORES * CORES) // CORES * SLABS + side) * parts
                first = side * columns * parts
                for part in range(parts):
                    ready[row, :, line + part, :] = held[
                        row, pair, pl.ds(first + part, columns, stride=parts), :
                    ]
                for index in range(columns):
                    place = place_order[row * columns + index]
                    if place != row * columns + index:
                        start = first + place % columns * parts
                        ready[row, index, line : line + parts, :] = held[
                            place // columns, pair, start : start + parts, :
                        ]
        copy = pltpu.make_async_copy(
            ready.at[row], out_ref.at[pl.ds(row * columns, columns)], out_sems.at[row]
        )
        copy.start()
        copies.append(copy)
    for copy in copies:
        copy.wait()


def split_bf16(value):
    high = value.astype(jnp.bfloat16)
    return high, (value - high.astype(jnp.float32)).astype(jnp.bfloat16)


def put_weights(moves, count_ref, held_refs, high_ref, low_ref):
    for index, ((core_move, slab_move), held_ref) in enumerate(zip(moves, held_refs)):
        cells, virt = held_ref.shape
        irrep = jnp.bitwise_xor(lax.axis_index("contract"), core_move)
        slab = jnp.bitwise_xor(lax.axis_index("redist"), slab_move)
        cell = lax.broadcasted_iota(jnp.int32, (cells, virt), 0)
        row, col = slab * (cells // VMAX) + cell // VMAX, cell % VMAX
        live = (row < count_ref[irrep]) & (col < count_ref[jnp.bitwise_xor(irrep, GAMMA)])
        high, low = split_bf16(jnp.where(live, 0.5 * held_ref[...], 0.0))
        high_ref[index * cells : (index + 1) * cells, :] = high
        low_ref[index * cells : (index + 1) * cells, :] = low


def weights_kernel(moves, count_ref, pair_energy_ref, virt_energy_ref, *refs):
    held_refs, (high_ref, low_ref, gap_ref) = refs[: len(moves)], refs[len(moves) :]
    put_weights(moves, count_ref, held_refs, high_ref, low_ref)
    gap_ref[...] = virt_energy_ref[...] - pair_energy_ref[0]


def last_weights_kernel(move, count_ref, held_ref, high_ref, low_ref):
    put_weights([move], count_ref, [held_ref], high_ref, low_ref)


def ladder_kernel(chip_order, moves, rows_ref, high_ref, low_ref, last_high_ref, last_low_ref, out_ref):
    places, lines, _ = rows_ref.shape
    virt = high_ref.shape[1]
    blocks = virt // VMAX
    turns = out_ref.shape[1] // blocks
    parts = last_high_ref.shape[0] // VMAX
    core = lax.axis_index("contract") % CORES
    side = lax.axis_index("redist") // RING % SLABS

    def arrived(source, slab_side):
        return jnp.concatenate(
            [
                jnp.concatenate(
                    [
                        rows_ref[:, ((source * turns + turn) * SLABS + slab_side) * parts + part, :]
                        for part in range(parts)
                    ],
                    axis=1,
                )
                for turn in range(turns)
            ],
            axis=0,
        )

    by_source = [[arrived(source, slab_side) for slab_side in range(SLABS)] for source in range(CORES)]
    by_core = [
        [jnp.where(core == 0, by_source[turn][place], by_source[1 - turn][place]) for place in range(SLABS)]
        for turn in range(CORES)
    ]
    by_move = {
        (turn, place * RING): jnp.where(side == 0, by_core[turn][place], by_core[turn][1 - place])
        for turn in range(CORES)
        for place in range(SLABS)
    }
    pieces = [by_move[move] for move in moves]
    total = jnp.zeros((turns * places, virt), jnp.float32)
    for rows, high, low in (
        (pieces[-1], last_high_ref[...], last_low_ref[...]),
        (jnp.concatenate(pieces[:-1], axis=1), high_ref[...], low_ref[...]),
    ):
        rows_high, rows_low = split_bf16(rows)
        total = total + jnp.dot(rows_high, low, preferred_element_type=jnp.float32)
        total = total + jnp.dot(rows_low, high, preferred_element_type=jnp.float32)
        total = total + jnp.dot(rows_high, high, preferred_element_type=jnp.float32)
    for index, turn in enumerate(chip_order):
        for block in range(blocks):
            out_ref[:, index * blocks + block, :] = total[
                turn * places : (turn + 1) * places, block * VMAX : (block + 1) * VMAX
            ]


def finish_kernel(parts_ref, gap_ref, out_ref):
    blocks = out_ref.shape[0]
    total = jnp.sum(parts_ref[...].reshape(-1, 2 * blocks, VMAX), axis=0)
    out_ref[...] = (total[:blocks] + total[blocks:]) / gap_ref[...]


def call(kernel, outs, in_memory, cost=None, out_memory=pltpu.VMEM, scratch=(), vmem_bytes=VMEM_BYTES):
    single = not isinstance(outs, list)
    shapes = [jax.ShapeDtypeStruct(*out) for out in ([outs] if single else outs)]
    specs = [pl.BlockSpec(memory_space=out_memory) for _ in shapes]
    return pl.pallas_call(
        kernel,
        out_shape=shapes[0] if single else shapes,
        in_specs=[pl.BlockSpec(memory_space=space) for space in in_memory],
        out_specs=specs[0] if single else specs,
        scratch_shapes=scratch,
        cost_estimate=cost,
        compiler_params=pltpu.CompilerParams(vmem_limit_bytes=vmem_bytes),
    )


def body(amplitudes, integrals, irrep_count, pair_energy, virt_energy):
    slabs = lax.axis_size("redist")
    owners = lax.axis_size("contract")
    pairs, _, cells_all = amplitudes.shape
    _, cells, virt = integrals.shape
    blocks = virt // VMAX
    places, chips = slabs // SLABS, owners // CORES
    vmem, smem = pltpu.VMEM, pltpu.SMEM
    f32, bf16 = jnp.float32, jnp.bfloat16

    def device(place, side, chip, core):
        row, column = divmod(place, RING)
        slab = (row * SLABS + (side ^ ((row + 1) // 2 % 2))) * RING + column
        return slab * owners + chip * CORES + core

    rows = places // RING
    place_order = first_swapped(places, rows // 2 * RING + RING // 2)
    chip_order = first_swapped(chips, chips // 2)
    same_chip = [
        [device(place, side, chip, core) for place in place_order for core in range(CORES)]
        for side in range(SLABS)
        for chip in range(chips)
    ]
    same_core = [
        [device(place, side, chip, core) for place in place_order for chip in chip_order]
        for side in range(SLABS)
        for core in range(CORES)
    ]

    def exchange(blocks_out, groups):
        return lax.all_to_all(
            blocks_out,
            ("redist", "contract"),
            split_axis=0,
            concat_axis=0,
            axis_index_groups=groups,
            tiled=True,
        )

    def swap(block, axis, move):
        count = lax.axis_size(axis)
        return lax.ppermute(block, axis, [(index, index ^ move) for index in range(count)])

    own = integrals.reshape(cells, virt)
    held = {(0, 0): own, (0, RING): swap(own, "redist", RING)}
    held |= {(1, move): swap(block, "contract", 1) for (_, move), block in held.items()}
    last_move, last_block = held.popitem()

    all_lines = cells_all // VMAX
    lines = pairs * all_lines // places
    grouped = call(
        functools.partial(regroup_kernel, place_order),
        ((places, lines, VMAX), f32),
        [pltpu.HBM],
        out_memory=pltpu.HBM,
        vmem_bytes=ALL_VMEM_BYTES,
        scratch=[
            pltpu.VMEM((rows, pairs, all_lines // rows, VMAX), f32),
            pltpu.VMEM((rows, RING, lines, VMAX), f32),
            pltpu.SemaphoreType.DMA((rows,)),
            pltpu.SemaphoreType.DMA((rows,)),
        ],
    )(amplitudes.reshape(pairs, all_lines, VMAX))
    arrived = exchange(grouped.reshape(places * CORES, lines // CORES, VMAX), same_chip)

    def weights(blocks_made):
        amount = blocks_made * cells * virt
        return (
            [((blocks_made * cells, virt), bf16)] * 2,
            pl.CostEstimate(flops=10 * amount, bytes_accessed=8 * amount, transcendentals=0),
        )

    outs, cost = weights(len(held))
    high, low, gap = call(
        functools.partial(weights_kernel, list(held)),
        [*outs, ((blocks, VMAX), f32)],
        [smem, smem, vmem] + [vmem] * len(held),
        cost=cost,
    )(irrep_count, pair_energy, virt_energy.reshape(blocks, VMAX), *held.values())
    outs, cost = weights(1)
    last_high, last_low = call(
        functools.partial(last_weights_kernel, last_move), outs, [smem, vmem], cost=cost
    )(irrep_count, last_block)

    partial = call(
        functools.partial(ladder_kernel, chip_order, [*held, last_move]),
        ((places, chips * blocks, VMAX), f32),
        [vmem] * 5,
    )(arrived.reshape(places, lines, VMAX), high, low, last_high, last_low)
    partial = exchange(partial.reshape(places * chips, blocks, VMAX), same_core)
    delta = call(finish_kernel, ((blocks, VMAX), f32), [vmem] * 2)(
        partial.reshape(-1, VMAX), gap
    )
    return delta.reshape(1, virt)


def solution(mesh):
    in_specs = (
        P("redist", "contract", None),
        P("contract", "redist", None),
        P(),
        P(("redist", "contract")),
        P(),
    )
    out_specs = P(("redist", "contract"), None)
    return jax.shard_map(body, mesh=mesh, in_specs=in_specs, out_specs=out_specs, check_vma=False)
```

```python
import functools

import jax
import jax.numpy as jnp
from jax import lax
from jax.experimental import pallas as pl
from jax.experimental.pallas import tpu as pltpu
from jax.sharding import PartitionSpec as P

VMAX = 128
GAMMA = 3
CORES = 2
SLABS = 2
RING = 8
VMEM_BYTES = 48 * 1024 * 1024
ALL_VMEM_BYTES = 63000000


def first_swapped(count, first):
    order = list(range(count))
    order[0], order[first] = first, 0
    return order


def regroup_kernel(place_order, cells_ref, out_ref, held, ready, in_sems, out_sems):
    pairs = cells_ref.shape[0]
    rows, columns, lines, _ = ready.shape
    parts = lines // pairs // SLABS
    row_lines = SLABS * columns * parts
    arrivals = [
        pltpu.make_async_copy(
            cells_ref.at[:, pl.ds(row * row_lines, row_lines), :], held.at[row], in_sems.at[row]
        )
        for row in range(rows)
    ]
    swapped = [row for row in range(rows) if place_order[row * columns] != row * columns]
    swapped += [place_order[row * columns] // columns for row in swapped]
    turns = sorted(range(rows), key=lambda row: row in swapped)
    for row in turns:
        arrivals[row].start()
    copies, waited = [], set()
    for row in turns:
        for needed in swapped if row in swapped else [row]:
            if needed not in waited:
                arrivals[needed].wait()
                waited.add(needed)
        for pair in range(pairs):
            for side in range(SLABS):
                line = ((pair % CORES * pairs + pair // CORES * CORES) // CORES * SLABS + side) * parts
                first = side * columns * parts
                for part in range(parts):
                    ready[row, :, line + part, :] = held[
                        row, pair, pl.ds(first + part, columns, stride=parts), :
                    ]
                for index in range(columns):
                    place = place_order[row * columns + index]
                    if place != row * columns + index:
                        start = first + place % columns * parts
                        ready[row, index, line : line + parts, :] = held[
                            place // columns, pair, start : start + parts, :
                        ]
        copy = pltpu.make_async_copy(
            ready.at[row], out_ref.at[pl.ds(row * columns, columns)], out_sems.at[row]
        )
        copy.start()
        copies.append(copy)
    for copy in copies:
        copy.wait()


def split_bf16(value):
    high = value.astype(jnp.bfloat16)
    return high, (value - high.astype(jnp.float32)).astype(jnp.bfloat16)


def put_weights(moves, count_ref, held_refs, high_ref, low_ref):
    for index, ((core_move, slab_move), held_ref) in enumerate(zip(moves, held_refs)):
        cells, virt = held_ref.shape
        irrep = jnp.bitwise_xor(lax.axis_index("contract"), core_move)
        slab = jnp.bitwise_xor(lax.axis_index("redist"), slab_move)
        cell = lax.broadcasted_iota(jnp.int32, (cells, virt), 0)
        row, col = slab * (cells // VMAX) + cell // VMAX, cell % VMAX
        live = (row < count_ref[irrep]) & (col < count_ref[jnp.bitwise_xor(irrep, GAMMA)])
        high, low = split_bf16(jnp.where(live, 0.5 * held_ref[...], 0.0))
        high_ref[index * cells : (index + 1) * cells, :] = high
        low_ref[index * cells : (index + 1) * cells, :] = low


def weights_kernel(moves, count_ref, pair_energy_ref, virt_energy_ref, *refs):
    held_refs, (high_ref, low_ref, gap_ref) = refs[: len(moves)], refs[len(moves) :]
    put_weights(moves, count_ref, held_refs, high_ref, low_ref)
    gap_ref[...] = virt_energy_ref[...] - pair_energy_ref[0]


def last_weights_kernel(move, count_ref, held_ref, high_ref, low_ref):
    put_weights([move], count_ref, [held_ref], high_ref, low_ref)


def ladder_kernel(chip_order, moves, rows_ref, high_ref, low_ref, last_high_ref, last_low_ref, out_ref):
    places, lines, _ = rows_ref.shape
    virt = high_ref.shape[1]
    blocks = virt // VMAX
    turns = out_ref.shape[1] // blocks
    parts = last_high_ref.shape[0] // VMAX
    core = lax.axis_index("contract") % CORES
    side = lax.axis_index("redist") // RING % SLABS

    def arrived(source, slab_side):
        return jnp.concatenate(
            [
                jnp.concatenate(
                    [
                        rows_ref[:, ((source * turns + turn) * SLABS + slab_side) * parts + part, :]
                        for part in range(parts)
                    ],
                    axis=1,
                )
                for turn in range(turns)
            ],
            axis=0,
        )

    by_source = [[arrived(source, slab_side) for slab_side in range(SLABS)] for source in range(CORES)]
    by_core = [
        [jnp.where(core == 0, by_source[turn][place], by_source[1 - turn][place]) for place in range(SLABS)]
        for turn in range(CORES)
    ]
    by_move = {
        (turn, place * RING): jnp.where(side == 0, by_core[turn][place], by_core[turn][1 - place])
        for turn in range(CORES)
        for place in range(SLABS)
    }
    pieces = [by_move[move] for move in moves]
    total = jnp.zeros((turns * places, virt), jnp.float32)
    for rows, high, low in (
        (pieces[-1], last_high_ref[...], last_low_ref[...]),
        (jnp.concatenate(pieces[:-1], axis=1), high_ref[...], low_ref[...]),
    ):
        rows_high, rows_low = split_bf16(rows)
        total = total + jnp.dot(rows_high, low, preferred_element_type=jnp.float32)
        total = total + jnp.dot(rows_low, high, preferred_element_type=jnp.float32)
        total = total + jnp.dot(rows_high, high, preferred_element_type=jnp.float32)
    for index, turn in enumerate(chip_order):
        for block in range(blocks):
            out_ref[:, index * blocks + block, :] = total[
                turn * places : (turn + 1) * places, block * VMAX : (block + 1) * VMAX
            ]


def finish_kernel(parts_ref, gap_ref, out_ref):
    blocks = out_ref.shape[0]
    total = jnp.sum(parts_ref[...].reshape(-1, 2 * blocks, VMAX), axis=0)
    out_ref[...] = (total[:blocks] + total[blocks:]) / gap_ref[...]


def call(kernel, outs, in_memory, cost=None, out_memory=pltpu.VMEM, scratch=(), vmem_bytes=VMEM_BYTES):
    single = not isinstance(outs, list)
    shapes = [jax.ShapeDtypeStruct(*out) for out in ([outs] if single else outs)]
    specs = [pl.BlockSpec(memory_space=out_memory) for _ in shapes]
    return pl.pallas_call(
        kernel,
        out_shape=shapes[0] if single else shapes,
        in_specs=[pl.BlockSpec(memory_space=space) for space in in_memory],
        out_specs=specs[0] if single else specs,
        scratch_shapes=scratch,
        cost_estimate=cost,
        compiler_params=pltpu.CompilerParams(vmem_limit_bytes=vmem_bytes),
    )


def body(amplitudes, integrals, irrep_count, pair_energy, virt_energy):
    slabs = lax.axis_size("redist")
    owners = lax.axis_size("contract")
    pairs, _, cells_all = amplitudes.shape
    _, cells, virt = integrals.shape
    blocks = virt // VMAX
    places, chips = slabs // SLABS, owners // CORES
    vmem, smem = pltpu.VMEM, pltpu.SMEM
    f32, bf16 = jnp.float32, jnp.bfloat16

    def device(place, side, chip, core):
        row, column = divmod(place, RING)
        slab = (row * SLABS + (side ^ ((row + 1) // 2 % 2))) * RING + column
        return slab * owners + chip * CORES + core

    rows = places // RING
    place_order = first_swapped(places, rows // 2 * RING + RING // 2 - 1)
    chip_order = first_swapped(chips, chips // 2)
    same_chip = [
        [device(place, side, chip, core) for place in place_order for core in range(CORES)]
        for side in range(SLABS)
        for chip in range(chips)
    ]
    same_core = [
        [device(place, side, chip, core) for place in place_order for chip in chip_order]
        for side in range(SLABS)
        for core in range(CORES)
    ]

    def exchange(blocks_out, groups):
        return lax.all_to_all(
            blocks_out,
            ("redist", "contract"),
            split_axis=0,
            concat_axis=0,
            axis_index_groups=groups,
            tiled=True,
        )

    def swap(block, axis, move):
        count = lax.axis_size(axis)
        return lax.ppermute(block, axis, [(index, index ^ move) for index in range(count)])

    own = integrals.reshape(cells, virt)
    held = {(0, 0): own, (0, RING): swap(own, "redist", RING)}
    held |= {(1, move): swap(block, "contract", 1) for (_, move), block in held.items()}
    last_move, last_block = held.popitem()

    all_lines = cells_all // VMAX
    lines = pairs * all_lines // places
    grouped = call(
        functools.partial(regroup_kernel, place_order),
        ((places, lines, VMAX), f32),
        [pltpu.HBM],
        out_memory=pltpu.HBM,
        vmem_bytes=ALL_VMEM_BYTES,
        scratch=[
            pltpu.VMEM((rows, pairs, all_lines // rows, VMAX), f32),
            pltpu.VMEM((rows, RING, lines, VMAX), f32),
            pltpu.SemaphoreType.DMA((rows,)),
            pltpu.SemaphoreType.DMA((rows,)),
        ],
    )(amplitudes.reshape(pairs, all_lines, VMAX))
    arrived = exchange(grouped.reshape(places * CORES, lines // CORES, VMAX), same_chip)

    def weights(blocks_made):
        amount = blocks_made * cells * virt
        return (
            [((blocks_made * cells, virt), bf16)] * 2,
            pl.CostEstimate(flops=10 * amount, bytes_accessed=8 * amount, transcendentals=0),
        )

    outs, cost = weights(len(held))
    high, low, gap = call(
        functools.partial(weights_kernel, list(held)),
        [*outs, ((blocks, VMAX), f32)],
        [smem, smem, vmem] + [vmem] * len(held),
        cost=cost,
    )(irrep_count, pair_energy, virt_energy.reshape(blocks, VMAX), *held.values())
    outs, cost = weights(1)
    last_high, last_low = call(
        functools.partial(last_weights_kernel, last_move), outs, [smem, vmem], cost=cost
    )(irrep_count, last_block)

    partial = call(
        functools.partial(ladder_kernel, chip_order, [*held, last_move]),
        ((places, chips * blocks, VMAX), f32),
        [vmem] * 5,
    )(arrived.reshape(places, lines, VMAX), high, low, last_high, last_low)
    partial = exchange(partial.reshape(places * chips, blocks, VMAX), same_core)
    delta = call(finish_kernel, ((blocks, VMAX), f32), [vmem] * 2)(
        partial.reshape(-1, VMAX), gap
    )
    return delta.reshape(1, virt)


def solution(mesh):
    in_specs = (
        P("redist", "contract", None),
        P("contract", "redist", None),
        P(),
        P(("redist", "contract")),
        P(),
    )
    out_specs = P(("redist", "contract"), None)
    return jax.shard_map(body, mesh=mesh, in_specs=in_specs, out_specs=out_specs, check_vma=False)
```
